512 devices in a mesh: dp: 64 (over y, z_lo, x), graph: 8 (over z_hi, core).
Axes of the slice: x: 4, y: 4, z: 16 (z_hi: 4, z_lo: 4; z = z_hi * 4 + z_lo), core: 2. Of those that a mesh axis runs over, the one named last changes fastest.
Arguments:
- node_emb: bfloat16 [64, 512, 512], P('dp', 'graph'), may hold values from -6 to 6
- edge_emb: bfloat16 [64, 64, 128, 512], P('dp', 'graph'), may hold values from -6 to 6
- edge_source: int32 [64, 64, 128], P('dp', 'graph'), may hold values from 0 to 511
- edge_target: int32 [64, 64, 128], P('dp', 'graph'), may hold values from 0 to 511
- valid_count: int32 [64, 64], P('dp', 'graph'), may hold values from 16 to 128
- triplets: int32 [64, 64, 2, 256], P('dp', 'graph'), may hold values from 0 to 127
- send_order: int32 [64, 8, 8], P('dp', 'graph'), may hold values from 0 to 7, each once within a row
- w_edge: bfloat16 [512, 512], replicated, may hold values from -0.25 to 0.25
- triplet_weight: bfloat16 [512, 512], replicated, may hold values from -0.25 to 0.25
- node_embedding_cotangent: bfloat16 [64, 512, 512], P('dp', 'graph'), may hold values from -6 to 6
Outputs:
- new_nodes: bfloat16 [64, 512, 512], P('dp', 'graph')
- new_edges: bfloat16 [64, 64, 128, 512], P('dp', 'graph')
- edge_projection_gradient: float32 [512, 512], replicated
- grad_trip: float32 [512, 512], replicated
The draws below stay inside these ranges and needn't reach their ends.
All inputs are finite; a program needn't handle non-finite values.
Results may differ from the reference program's by a relative error of at most 0.0095.
Values may be sent and summed in bfloat16 or wider, within the bound.
A program may use at most 64 MiB of HBM per device.

```python
import math
import jax
import jax.numpy as jnp
from jax import lax

D = 512
EB = 128
TRIP = 256
BLK_DEV = 8
NODES = 512
EDGE_BLOCK_COUNT = 64
N_DP = 64
N_GRAPH = 8


def plant(entries, stream_key, least, top_value):
    spot = [jax.random.randint(jax.random.fold_in(stream_key, axis), (), 0, length) for axis, length in enumerate(entries.shape)]
    longest = entries.shape.index(max(entries.shape))
    neighbour = spot[:longest] + [(spot[longest] + 1) % entries.shape[longest]] + spot[longest + 1:]
    return entries.at[tuple(spot)].set(least).at[tuple(neighbour)].set(top_value)


def block_levels(stream_key, dims, shards, least, top_value):
    def one(position, parts):
        heights = jax.random.uniform(jax.random.fold_in(jax.random.fold_in(stream_key, 6), position), (parts,), jnp.float32, least / len(shards), top_value / len(shards))
        return jnp.repeat(jnp.exp(heights), dims[position] // parts).reshape((-1,) + (1,) * (len(dims) - position - 1))

    gain = one(*shards[0])
    for cut in shards[1:]:
        gain = gain * one(*cut)
    return gain


def gaussian(rng, shape, deviation, reach, pieces=(), kind=jnp.bfloat16):
    values = jax.random.normal(rng, shape, jnp.float32) * deviation
    if len(pieces) > 0:
        values = block_levels(rng, shape, pieces, -0.22, 0.18) * values
    return jnp.clip(values, min=-reach, max=reach).astype(kind)


def setup_inputs(seed: int = 0) -> dict:
    key_list = jax.random.split(jax.random.key(seed), 11)
    node_emb = gaussian(key_list[0], (N_DP, NODES, D), 1.0, 6.0, ((0, 64), (1, 8)))
    edge_emb = gaussian(key_list[1], (N_DP, EDGE_BLOCK_COUNT, EB, D), 1.0, 6.0, ((0, 64), (1, 8)))
    edge_source = plant(jax.random.randint(key_list[2], (N_DP, EDGE_BLOCK_COUNT, EB), 0, NODES), jax.random.fold_in(key_list[2], 1), 0, NODES - 1).astype(jnp.int32)
    edge_target = plant(jax.random.randint(key_list[3], (N_DP, EDGE_BLOCK_COUNT, EB), 0, NODES), jax.random.fold_in(key_list[3], 1), 0, NODES - 1).astype(jnp.int32)
    valid_count = plant(jax.random.randint(key_list[4], (N_DP, EDGE_BLOCK_COUNT), 16, 129), jax.random.fold_in(key_list[4], 1), 16, 128).astype(jnp.int32)
    triplets = plant(jax.random.randint(key_list[5], (N_DP, EDGE_BLOCK_COUNT, 2, TRIP), 0, EB), jax.random.fold_in(key_list[5], 1), 0, EB - 1).astype(jnp.int32)
    send_order = jax.vmap(lambda own: jax.random.permutation(own, BLK_DEV))(jax.random.split(key_list[6], N_DP * N_GRAPH)).reshape((N_DP, N_GRAPH, BLK_DEV)).astype(jnp.int32)
    w_edge = gaussian(key_list[7], (D, D), D ** -0.5, 0.25)
    triplet_weight = gaussian(key_list[8], (D, D), D ** -0.5, 0.25)
    node_embedding_cotangent = gaussian(key_list[9], (N_DP, NODES, D), 1.0, 6.0, ((0, 64), (1, 8)))
    return {"node_emb": node_emb, "edge_emb": edge_emb, "edge_source": edge_source, "edge_target": edge_target, "valid_count": valid_count, "triplets": triplets, "send_order": send_order, "w_edge": w_edge, "triplet_weight": triplet_weight, "node_embedding_cotangent": node_embedding_cotangent}


def single_batch(items, w_edge, triplet_weight):
    node_b, emb_b, src_b, dst_b, cnt_b, trip_b, order_b, cot_b = items
    per = BLK_DEV // N_GRAPH
    offsets = order_b + BLK_DEV * jnp.arange(N_GRAPH, dtype=jnp.int32)[:, None]
    perm = offsets.reshape(N_GRAPH, N_GRAPH, per).transpose(1, 0, 2).reshape(-1).astype(jnp.int32)
    emb = emb_b[perm]
    src = src_b[perm].reshape(-1)
    dst = dst_b[perm].reshape(-1)
    cnt = cnt_b[perm]
    trip = trip_b[perm]
    blocks = EDGE_BLOCK_COUNT
    edges = blocks * EB
    slot = lax.broadcasted_iota(jnp.int32, (blocks, EB), 1)
    mask = (slot < cnt[:, None]).astype(jnp.float32).reshape(edges, 1)
    flat = emb.reshape(edges, D)
    x = (flat.astype(jnp.float32) + node_b[src].astype(jnp.float32) + node_b[dst].astype(jnp.float32)).astype(jnp.bfloat16)
    z = jnp.dot(x, w_edge, preferred_element_type=jnp.float32)
    sig = jax.nn.sigmoid(z)
    u = (mask * z * sig).astype(jnp.bfloat16)
    y = jnp.dot(u, triplet_weight, preferred_element_type=jnp.float32).astype(jnp.bfloat16)
    cols = jnp.arange(EB, dtype=jnp.int32)
    single_receiver = (trip[:, 0, :, None] == cols).astype(jnp.float32)
    single_sender = (trip[:, 1, :, None] == cols).astype(jnp.float32)
    edge_connections = jnp.einsum('can,cag->cng', single_receiver, single_sender).astype(jnp.bfloat16)
    t = jnp.einsum('kpq,kqd->kpd', edge_connections.astype(jnp.float32), y.reshape(blocks, EB, D).astype(jnp.float32)).reshape(edges, D)
    v = (mask * (u.astype(jnp.float32) + t)).astype(jnp.bfloat16)
    new_edges = (flat.astype(jnp.float32) + v.astype(jnp.float32)).astype(jnp.bfloat16).reshape(blocks, EB, D)
    agg = jax.ops.segment_sum(v.astype(jnp.float32), dst, num_segments=NODES)
    new_nodes = (node_b.astype(jnp.float32) + 0.25 * agg).astype(jnp.bfloat16)
    coef = 0.25 / math.sqrt(N_DP * NODES)
    dv = (mask * cot_b[dst].astype(jnp.float32) * coef).astype(jnp.bfloat16)
    dy = jnp.einsum('kqp,kqd->kpd', edge_connections.astype(jnp.float32), dv.reshape(blocks, EB, D).astype(jnp.float32)).reshape(edges, D).astype(jnp.bfloat16)
    du = dv.astype(jnp.float32) + jnp.dot(dy, triplet_weight.T, preferred_element_type=jnp.float32)
    dz = (du * mask * sig * (1.0 + z * (1.0 - sig))).astype(jnp.bfloat16)
    g_edge = jnp.dot(x.T, dz, preferred_element_type=jnp.float32)
    g_trip = jnp.dot(u.T, dy, preferred_element_type=jnp.float32)
    return (new_nodes, new_edges, g_edge, g_trip)

def reference(node_emb, edge_emb, edge_source, edge_target, valid_count, triplets, send_order, w_edge, triplet_weight, node_embedding_cotangent):
    items = (node_emb, edge_emb, edge_source, edge_target, valid_count, triplets, send_order, node_embedding_cotangent)
    new_nodes, new_edges, g_edge, g_trip = lax.map(lambda one: single_batch(one, w_edge, triplet_weight), items)
    return (new_nodes, new_edges, lax.optimization_barrier(jnp.sum(g_edge, axis=0)), lax.optimization_barrier(jnp.sum(g_trip, axis=0)))
```

```python
import math

import jax
import jax.numpy as jnp
from jax import lax
from jax.experimental import pallas as pl
from jax.experimental.pallas import tpu as pltpu
from jax.sharding import PartitionSpec as P

MESH = pl.DeviceIdType.MESH
F32, BF16 = jnp.float32, jnp.bfloat16

Q = 4
BLK, SLOTS, WIDTH, NODES = 8, 128, 512, 512
OWN = NODES // 8
ROUTE = ((2, 0), (2, 1), (1, 0), (1, 1), (3, 0), (3, 1), (0, 1), (0, 0))


def dot(a, b, ca, cb):
    return lax.dot_general(a, b, (((ca,), (cb,)), ((), ())), preferred_element_type=F32)


def kernel(
    coef,
    order,
    count,
    src_in,
    dst_in,
    trip_in,
    node_in,
    cot_in,
    emb_in,
    w_in,
    tw_in,
    nodes_out,
    edges_out,
    grads_out,
    srcs,
    dsts,
    trips,
    node,
    cot,
    emb,
    w,
    tw,
    pick,
    pick_t,
    spread,
    links,
    links_t,
    xs,
    us,
    ys,
    fs,
    vs,
    dzs,
    far,
    near,
    relay,
    agg_sib_out,
    agg_sib_in,
    agg,
    agg_one_out,
    agg_one_in,
    agg_two_out,
    agg_two_in,
    grads,
    gs_out,
    gs_in,
    r1_out,
    r1_in,
    r1_sum,
    r2_out,
    r2_in,
    r3_out,
    r3_in,
    r4,
    total,
    lsem,
    ssem,
    rsem,
):
    g, d = lax.axis_index("graph"), lax.axis_index("dp")
    h, c = g // 2, g % 2
    y, zl, x = d // 16, (d // 4) % 4, d % 4

    def peer(dh, dc):
        return (d, ((h + dh) % 4) * 2 + (c + dc) % 2)

    def at(yy, zz, xx):
        return (((yy % 4) * 4 + zz % 4) * 4 + xx % 4, g)

    def first(i):
        return at(y + i * c, zl, x + i * (1 - c))

    def second(i):
        return at(y + i * (1 - c), zl, x + i * c)

    def third(i):
        return at(y, zl + i, x)

    p = x * (1 - c) + y * c
    s = y * (1 - c) + x * c

    used = [0]

    def send(source, target, device):
        i = used[0]
        used[0] += 1
        copy = pltpu.make_async_remote_copy(
            src_ref=source,
            dst_ref=target,
            send_sem=ssem.at[i],
            recv_sem=rsem.at[i],
            device_id=device,
            device_id_type=MESH,
        )
        copy.start()
        return copy

    local = [0]

    def fetch(source, target):
        copy = pltpu.make_async_copy(source, target, lsem.at[local[0]])
        local[0] += 1
        copy.start()
        return copy

    def rows(i, n):
        return pl.ds(pl.multiple_of(i * n, n), n)

    own = rows(g, OWN)
    in_node = fetch(node_in, node.at[own])
    in_ids = [fetch(src_in, srcs), fetch(dst_in, dsts), fetch(trip_in, trips)]
    in_cot = fetch(cot_in, cot.at[own])
    in_emb = fetch(emb_in, emb)
    in_w = [fetch(w_in, w), fetch(tw_in, tw)]

    partners = [peer(0, 1), peer(1, 0), peer(1, 1), peer(3, 0), peer(3, 1), peer(2, 0)]
    for i in (1, 2, 3):
        partners += [first(i), second(i), third(i)]
    barrier = pltpu.get_barrier_semaphore()
    for partner in partners:
        pl.semaphore_signal(barrier, 1, device_id=partner, device_id_type=MESH)
    pl.semaphore_wait(barrier, len(partners))

    ended = []

    def part(ref, dh, dc, half=None):
        base = (((h + dh) % 4) * 2 + (c + dc) % 2) * OWN
        if half is None:
            return ref.at[pl.ds(pl.multiple_of(base, OWN), OWN)]
        return ref.at[pl.ds(pl.multiple_of(base + half * (OWN // 2), OWN // 2), OWN // 2)]

    def gather_one(ref):
        return [send(part(ref, 0, 0), part(ref, 0, 0), peer(*to)) for to in ((1, 0), (3, 0), (0, 1))]

    def gather_two(ref, one):
        up, down, beside = one
        up.wait_recv()
        two = [
            send(part(ref, 3, 0, 0), part(ref, 3, 0, 0), peer(1, 0)),
            send(part(ref, 3, 0), part(ref, 3, 0), peer(0, 1)),
        ]
        down.wait_recv()
        two += [
            send(part(ref, 1, 0, 1), part(ref, 1, 0, 1), peer(3, 0)),
            send(part(ref, 1, 0), part(ref, 1, 0), peer(0, 1)),
        ]
        return two

    def gather_three(ref, one, two):
        two[0].wait_recv()
        three = [send(part(ref, 2, 0, 0), part(ref, 2, 0, 0), peer(0, 1))]
        two[2].wait_recv()
        three += [send(part(ref, 2, 0, 1), part(ref, 2, 0, 1), peer(0, 1))]
        ended.extend(one + two + three)
        return [one[2], two[1], two[3]] + three

    in_node.wait()
    node_one = gather_one(node)
    for copy in in_ids:
        copy.wait()

    lane = lax.broadcasted_iota(jnp.int32, (SLOTS, SLOTS), 1)
    sub = lax.broadcasted_iota(jnp.int32, (SLOTS, SLOTS), 0)
    sub_wide = lax.broadcasted_iota(jnp.int32, (SLOTS, 2 * SLOTS), 0)

    def block(r):
        dh, dc = ROUTE[r]
        return order[((h + dh) % 4) * 2 + (c + dc) % 2]

    def prepare(r):
        b = block(r)
        here = pl.ds(r * SLOTS, SLOTS)
        source = jnp.broadcast_to(srcs[pl.ds(b, 1), :], (SLOTS, SLOTS))
        target = jnp.broadcast_to(dsts[pl.ds(b, 1), :], (SLOTS, SLOTS))
        source_t, target_t = source.T, target.T
        for j in range(NODES // SLOTS):
            columns = pl.ds(j * SLOTS, SLOTS)
            from_ = jnp.where(source_t == lane + j * SLOTS, 1.0, 0.0)
            to = jnp.where(target_t == lane + j * SLOTS, 1.0, 0.0)
            pick[here, columns] = (from_ + to).astype(BF16)
            pick_t[here, columns] = to.astype(BF16)
            spread[columns, here] = jnp.where(target == sub + j * SLOTS, 1.0, 0.0).astype(BF16)
        pair = trips[b]
        receive = jnp.where(pair[0:1, :] == sub_wide, 1.0, 0.0).astype(BF16)
        sender = jnp.where(pair[1:2, :] == sub_wide, 1.0, 0.0).astype(BF16)
        links[r] = dot(receive, sender, 1, 1).astype(BF16)
        links_t[r] = dot(sender, receive, 1, 1).astype(BF16)

    for r in range(2):
        prepare(r)
    in_cot.wait()
    in_emb.wait()
    for copy in in_w:
        copy.wait()
    node_two = gather_two(node, node_one)
    cot_one = gather_one(cot)
    for r in range(2, 8):
        prepare(r)
    for copy in gather_three(node, node_one, node_two):
        copy.wait_recv()

    def live(r):
        rows_ = lax.broadcasted_iota(jnp.int32, (SLOTS, WIDTH), 0)
        return jnp.where(rows_ < count[block(r)], 1.0, 0.0)

    def forward(t):
        here = pl.ds(t * 2 * SLOTS, 2 * SLOTS)
        flat = jnp.concatenate([emb[block(2 * t + i)] for i in range(2)], axis=0).astype(F32)
        mask = jnp.concatenate([live(2 * t + i) for i in range(2)], axis=0)
        x_ = (flat + dot(pick[here, :], node[...], 1, 0)).astype(BF16)
        xs[here, :] = x_
        z = dot(x_, w[...], 1, 0)
        sig = jax.nn.sigmoid(z)
        u = (mask * z * sig).astype(BF16)
        us[here, :] = u
        fs[here, :] = mask * sig * (1.0 + z * (1.0 - sig))
        y_ = dot(u, tw[...], 1, 0).astype(BF16)
        moved = jnp.concatenate(
            [dot(links[2 * t + i], y_[i * SLOTS : (i + 1) * SLOTS], 1, 0) for i in range(2)], axis=0
        )
        v = (mask * (u.astype(F32) + moved)).astype(BF16)
        vs[here, :] = v
        return (flat + v.astype(F32)).astype(BF16)

    half = SLOTS // 2
    made = forward(0)
    for i in range(2):
        for j in range(2):
            far[j, i] = made[i * SLOTS + j * half : i * SLOTS + (j + 1) * half]
    hops = [send(far.at[0], relay.at[0], peer(1, 0)), send(far.at[1], relay.at[1], peer(3, 0))]

    cot_two = gather_two(cot, cot_one)
    direct = []

    def hand_out(t):
        made = forward(t)
        for i in range(2):
            r = 2 * t + i
            near[r - 2] = made[i * SLOTS : (i + 1) * SLOTS]
            if r == 7:
                return direct.append(fetch(near.at[r - 2], edges_out.at[g]))
            direct.append(send(near.at[r - 2], edges_out.at[g], peer(*ROUTE[r])))

    hand_out(1)
    hand_out(2)
    cot_in_all = gather_three(cot, cot_one, cot_two)
    hand_out(3)

    agg[...] = dot(spread[...], vs[...], 1, 0)
    for i in range(4):
        agg_sib_out[pl.ds(i * OWN, OWN)] = agg[rows(2 * i + 1 - c, OWN)].astype(BF16)
    agg_sib = send(agg_sib_out, agg_sib_in, peer(0, 1))

    for copy in cot_in_all:
        copy.wait_recv()
    for t in range(4):
        here = pl.ds(t * 2 * SLOTS, 2 * SLOTS)
        mask = jnp.concatenate([live(2 * t + i) for i in range(2)], axis=0)
        dv = (mask * dot(pick_t[here, :], cot[...], 1, 0) * coef).astype(BF16)
        dy = jnp.concatenate(
            [dot(links_t[2 * t + i], dv[i * SLOTS : (i + 1) * SLOTS], 1, 0) for i in range(2)], axis=0
        ).astype(BF16)
        ys[here, :] = dy
        du = dv.astype(F32) + dot(dy, tw[...], 1, 1)
        dzs[here, :] = (du * fs[here, :]).astype(BF16)

    grads[0] = dot(xs[...], dzs[...], 0, 0)
    grads[1] = dot(us[...], ys[...], 0, 0)
    gs_out[...] = grads[1 - c].astype(BF16)
    grad_sib = send(gs_out, gs_in, peer(0, 1))

    agg_sib.wait_recv()

    def chip_sum(dh, half=None):
        i = (h + dh) % 4
        n = OWN if half is None else OWN // 2
        o = 0 if half is None else half * (OWN // 2)
        mine = agg[pl.ds(pl.multiple_of((2 * i + c) * OWN + o, n), n)]
        return mine + agg_sib_in[pl.ds(pl.multiple_of(i * OWN + o, n), n)].astype(F32)

    for i in range(2):
        agg_one_out[i] = chip_sum(2, i).astype(BF16)
    agg_one = [send(agg_one_out.at[0], agg_one_in.at[0], peer(1, 0)),
               send(agg_one_out.at[1], agg_one_in.at[1], peer(3, 0))]

    grad_sib.wait_recv()
    grads[c] = grads[c] + gs_in[...].astype(F32)
    red_one = []
    for i in (1, 2, 3):
        r1_out[i - 1] = grads[c, rows((p + i) % 4, 128), :].astype(BF16)
        red_one.append(send(r1_out.at[i - 1], r1_in.at[i - 1], first(i)))

    for i in range(2):
        hops[i].wait_recv()
        to = (1, 3)[i]
        slot = ((h + 4 - to) % 4) * 2 + c
        for j in range(2):
            direct.append(
                send(relay.at[i, j], edges_out.at[slot, pl.ds(i * half, half)], peer(to, j))
            )

    for i in range(2):
        agg_one[i].wait_recv()
        agg_two_out[i, pl.ds(i * (OWN // 2), OWN // 2)] = (
            chip_sum((1, 3)[i], i) + agg_one_in[i].astype(F32)
        ).astype(BF16)
        agg_two_out[i, pl.ds((1 - i) * (OWN // 2), OWN // 2)] = chip_sum((1, 3)[i], 1 - i).astype(BF16)
    agg_two = [send(agg_two_out.at[i], agg_two_in.at[i], peer((1, 3)[i], 0)) for i in range(2)]

    for copy in red_one:
        copy.wait_recv()
    r1_sum[...] = (
        grads[c, rows(p, 128), :] + r1_in[0].astype(F32) + r1_in[1].astype(F32) + r1_in[2].astype(F32)
    )
    red_two = []
    for i in (1, 2, 3):
        r2_out[i - 1] = r1_sum[rows((s + i) % 4, 32), :].astype(BF16)
        red_two.append(send(r2_out.at[i - 1], r2_in.at[i - 1], second(i)))
    for copy in red_two:
        copy.wait_recv()
    r2 = r1_sum[rows(s, 32), :]
    for i in range(3):
        r2 = r2 + r2_in[i].astype(F32)
    for i in range(4):
        r3_out[i] = r2[:, i * 128 : (i + 1) * 128]
    red_three = []
    for i in (1, 2, 3):
        k = (zl + i) % 4
        r3_in[i + 2] = r3_out[k].astype(BF16)
        red_three.append(send(r3_in.at[i + 2], r3_in.at[i - 1], third(i)))
    for copy in red_three:
        copy.wait_recv()
    r3 = r3_out[zl]
    for i in range(3):
        r3 = r3 + r3_in[i].astype(F32)
    r4[h] = r3.astype(BF16)
    red_four = [send(r4.at[h], r4.at[h], peer(i, 0)) for i in (1, 2, 3)]

    for copy in agg_two:
        copy.wait_recv()
    nodes_out[...] = (
        node[own].astype(F32)
        + 0.25 * (chip_sum(0) + agg_two_in[0].astype(F32) + agg_two_in[1].astype(F32))
    ).astype(BF16)

    for copy in red_four:
        copy.wait_recv()
    four = r4[0].astype(F32) + r4[1].astype(F32) + r4[2].astype(F32) + r4[3].astype(F32)
    block_ = pl.ds(pl.multiple_of(p * 128 + s * 32, 32), 32)
    band = pl.ds(pl.multiple_of(zl * 128, 128), 128)
    total[c, block_, band] = four.astype(BF16)

    def spread_out(region, partner):
        return [send(total.at[region], total.at[region], partner(i)) for i in (1, 2, 3)]

    back = spread_out((c, block_, band), third)
    for copy in back:
        copy.wait_recv()
    back_two = spread_out((c, block_), second)
    for copy in back_two:
        copy.wait_recv()
    back_one = spread_out((c, rows(p, 128)), first)
    for copy in back_one:
        copy.wait_recv()
    last = send(total.at[c], total.at[c], peer(0, 1))
    last.wait_recv()
    grads_out[...] = total[...]

    for copy in direct:
        if copy is direct[5]:
            copy.wait()
        else:
            copy.wait_recv()
    for i, copy in enumerate(direct):
        if i != 5:
            copy.wait_send()
    for copy in (
        ended + hops + [agg_sib, grad_sib] + agg_one + agg_two + red_one + red_two + red_three
        + red_four + back + back_two + back_one + [last]
    ):
        copy.wait_send()


def shards(
    node_emb,
    edge_emb,
    edge_source,
    edge_target,
    valid_count,
    triplets,
    send_order,
    w_edge,
    triplet_weight,
    node_embedding_cotangent,
):
    coef = 0.25 / math.sqrt(lax.axis_size("dp") * NODES)
    anywhere = pl.BlockSpec(memory_space=pl.ANY)
    smem = pl.BlockSpec(memory_space=pltpu.SMEM)
    vmem = pl.BlockSpec(memory_space=pltpu.VMEM)
    edges = BLK * SLOTS
    half = SLOTS // 2

    def scratch(*shape, dtype=BF16):
        return pltpu.VMEM(shape, dtype)

    nodes, packed, grads = pl.pallas_call(
        lambda *refs: kernel(coef, *refs),
        out_shape=(
            jax.ShapeDtypeStruct((OWN, WIDTH), BF16),
            jax.ShapeDtypeStruct((BLK, SLOTS, WIDTH), BF16),
            jax.ShapeDtypeStruct((2, WIDTH, WIDTH), BF16),
        ),
        in_specs=[smem, smem] + [anywhere] * 8,
        out_specs=(vmem, anywhere, vmem),
        scratch_shapes=[
            scratch(BLK, SLOTS, dtype=jnp.int32),
            scratch(BLK, SLOTS, dtype=jnp.int32),
            scratch(BLK, 2, 2 * SLOTS, dtype=jnp.int32),
            scratch(NODES, WIDTH),
            scratch(NODES, WIDTH),
            scratch(BLK, SLOTS, WIDTH),
            scratch(WIDTH, WIDTH),
            scratch(WIDTH, WIDTH),
            scratch(edges, NODES),
            scratch(edges, NODES),
            scratch(NODES, edges),
            scratch(BLK, SLOTS, SLOTS),
            scratch(BLK, SLOTS, SLOTS),
            scratch(edges, WIDTH),
            scratch(edges, WIDTH),
            scratch(edges, WIDTH),
            scratch(edges, WIDTH, dtype=F32),
            scratch(edges, WIDTH),
            scratch(edges, WIDTH),
            scratch(2, 2, half, WIDTH),
            scratch(6, SLOTS, WIDTH),
            scratch(2, 2, half, WIDTH),
            scratch(4 * OWN, WIDTH),
            scratch(4 * OWN, WIDTH),
            scratch(NODES, WIDTH, dtype=F32),
            scratch(2, OWN // 2, WIDTH),
            scratch(2, OWN // 2, WIDTH),
            scratch(2, OWN, WIDTH),
            scratch(2, OWN, WIDTH),
            scratch(2, WIDTH, WIDTH, dtype=F32),
            scratch(WIDTH, WIDTH),
            scratch(WIDTH, WIDTH),
            scratch(3, 128, WIDTH),
            scratch(3, 128, WIDTH),
            scratch(128, WIDTH, dtype=F32),
            scratch(3, 32, WIDTH),
            scratch(3, 32, WIDTH),
            scratch(4, 32, 128, dtype=F32),
            scratch(6, 32, 128),
            scratch(4, 32, 128),
            scratch(2, WIDTH, WIDTH),
            pltpu.SemaphoreType.DMA((9,)),
            pltpu.SemaphoreType.DMA((64,)),
            pltpu.SemaphoreType.DMA((64,)),
        ],
        compiler_params=pltpu.CompilerParams(
            collective_id=0, has_side_effects=True, vmem_limit_bytes=48 << 20
        ),
    )(
        send_order.reshape(BLK),
        valid_count.reshape(BLK),
        edge_source[0],
        edge_target[0],
        triplets[0],
        node_emb[0],
        node_embedding_cotangent[0],
        edge_emb[0],
        w_edge,
        triplet_weight,
    )
    return (nodes[None], packed[None], grads[0].astype(F32), grads[1].astype(F32))


def solution(mesh):
    in_specs = (
        P("dp", "graph", None),
        P("dp", "graph", None, None),
        P("dp", "graph", None),
        P("dp", "graph", None),
        P("dp", "graph"),
        P("dp", "graph", None, None),
        P("dp", "graph", None),
        P(),
        P(),
        P("dp", "graph", None),
    )
    out_specs = (P("dp", "graph", None), P("dp", "graph", None, None), P(), P())
    return jax.shard_map(shards, mesh=mesh, in_specs=in_specs, out_specs=out_specs, check_vma=False)
```

```python
import math

import jax
import jax.numpy as jnp
from jax import lax
from jax.experimental import pallas as pl
from jax.experimental.pallas import tpu as pltpu
from jax.sharding import PartitionSpec as P

MESH = pl.DeviceIdType.MESH
F32, BF16 = jnp.float32, jnp.bfloat16

TILE = 32
BLK, SLOTS, WIDTH, NODES = 8, 128, 512, 512
OWN = NODES // 8
ROUTE = ((2, 0), (2, 1), (1, 0), (1, 1), (3, 0), (3, 1), (0, 1), (0, 0))


class Copy:
    def __init__(self, copy, remote=True):
        self.copy, self.remote, self.got, self.left = copy, remote, False, False

    def wait_recv(self):
        if not self.got:
            self.copy.wait_recv() if self.remote else self.copy.wait()
            self.got = True

    wait = wait_recv

    def wait_send(self):
        if self.remote and not self.left:
            self.copy.wait_send()
            self.left = True


def dot(a, b, ca, cb):
    return lax.dot_general(a, b, (((ca,), (cb,)), ((), ())), preferred_element_type=F32)


def kernel(
    coef,
    order,
    count,
    src_in,
    dst_in,
    trip_in,
    node_in,
    cot_in,
    emb_in,
    w_in,
    tw_in,
    nodes_out,
    edges_out,
    grads_out,
    srcs,
    dsts,
    trips,
    node,
    cot,
    emb,
    w,
    tw,
    pick,
    pick_t,
    spread,
    links,
    links_t,
    left,
    right,
    fs,
    vs,
    dvs,
    tmp,
    near,
    agg_sib_out,
    agg_sib_in,
    agg,
    agg_one_out,
    agg_one_in,
    agg_two_out,
    agg_two_in,
    grads,
    gs_out,
    gs_in,
    r1_out,
    r1_in,
    r1_sum,
    r2_out,
    r2_in,
    r3_out,
    r3_in,
    r4,
    total,
    lsem,
    ssem,
    rsem,
):
    g, d = lax.axis_index("graph"), lax.axis_index("dp")
    h, c = g // 2, g % 2
    y, zl, x = d // 16, (d // 4) % 4, d % 4

    def peer(dh, dc):
        return (d, ((h + dh) % 4) * 2 + (c + dc) % 2)

    def at(yy, zz, xx):
        return (((yy % 4) * 4 + zz % 4) * 4 + xx % 4, g)

    def first(i):
        return at(y + i * c, zl, x + i * (1 - c))

    def second(i):
        return at(y + i * (1 - c), zl, x + i * c)

    def third(i):
        return at(y, zl + i, x)

    p = x * (1 - c) + y * c
    s = y * (1 - c) + x * c

    used = [0]
    every = []

    def finish():
        for copy in every:
            copy.wait_recv()
        for copy in every:
            copy.wait_send()


    def send(source, target, device):
        i = used[0]
        used[0] += 1
        copy = pltpu.make_async_remote_copy(
            src_ref=source,
            dst_ref=target,
            send_sem=ssem.at[i],
            recv_sem=rsem.at[i],
            device_id=device,
            device_id_type=MESH,
        )
        copy.start()
        copy = Copy(copy)
        every.append(copy)
        return copy

    local = [0]

    def fetch(source, target):
        copy = pltpu.make_async_copy(source, target, lsem.at[local[0]])
        local[0] += 1
        copy.start()
        copy = Copy(copy, False)
        every.append(copy)
        return copy

    def rows(i, n):
        return pl.ds(pl.multiple_of(i * n, n), n)

    own = rows(g, OWN)
    in_node = fetch(node_in, node.at[own])
    in_ids = [fetch(src_in, srcs), fetch(dst_in, dsts), fetch(trip_in, trips)]
    in_cot = fetch(cot_in, cot.at[own])
    in_emb = fetch(emb_in, emb)
    in_w = [fetch(w_in, w), fetch(tw_in, tw)]

    partners = [peer(0, 1), peer(1, 0), peer(1, 1), peer(3, 0), peer(3, 1), peer(2, 0), peer(2, 1)]
    for i in (1, 2, 3):
        partners += [first(i), second(i), third(i)]
    barrier = pltpu.get_barrier_semaphore()
    for partner in partners:
        pl.semaphore_signal(barrier, 1, device_id=partner, device_id_type=MESH)
    pl.semaphore_wait(barrier, len(partners))


    def part(ref, dh, dc, half=None):
        base = (((h + dh) % 4) * 2 + (c + dc) % 2) * OWN
        if half is None:
            return ref.at[pl.ds(pl.multiple_of(base, OWN), OWN)]
        return ref.at[pl.ds(pl.multiple_of(base + half * (OWN // 2), OWN // 2), OWN // 2)]

    def gather_one(ref):
        return [send(part(ref, 0, 0), part(ref, 0, 0), peer(*to)) for to in ((1, 0), (3, 0), (0, 1))]

    def gather_two(ref, one):
        up, down, beside = one
        up.wait_recv()
        two = [
            send(part(ref, 3, 0, 0), part(ref, 3, 0, 0), peer(1, 0)),
            send(part(ref, 3, 0), part(ref, 3, 0), peer(0, 1)),
        ]
        down.wait_recv()
        two += [
            send(part(ref, 1, 0, 1), part(ref, 1, 0, 1), peer(3, 0)),
            send(part(ref, 1, 0), part(ref, 1, 0), peer(0, 1)),
        ]
        return two

    def gather_three(ref, one, two):
        two[0].wait_recv()
        three = [send(part(ref, 2, 0, 0), part(ref, 2, 0, 0), peer(0, 1))]
        two[2].wait_recv()
        three += [send(part(ref, 2, 0, 1), part(ref, 2, 0, 1), peer(0, 1))]
        return [one[2], two[1], two[3]] + three

    in_node.wait()
    node_one = gather_one(node)
    in_cot.wait()
    cot_one = gather_one(cot)
    for copy in in_ids:
        copy.wait()

    lane = lax.broadcasted_iota(jnp.int32, (SLOTS, SLOTS), 1)
    sub = lax.broadcasted_iota(jnp.int32, (SLOTS, SLOTS), 0)
    sub_wide = lax.broadcasted_iota(jnp.int32, (SLOTS, 2 * SLOTS), 0)

    def block(r):
        dh, dc = ROUTE[r]
        return order[((h + dh) % 4) * 2 + (c + dc) % 2]

    def prepare(r):
        b = block(r)
        alive = count[b]
        here = pl.ds(r * SLOTS, SLOTS)
        live = lax.broadcasted_iota(jnp.int32, (1, SLOTS), 1) < alive
        source = jnp.broadcast_to(jnp.where(live, srcs[pl.ds(b, 1), :], -1), (SLOTS, SLOTS))
        target = jnp.broadcast_to(jnp.where(live, dsts[pl.ds(b, 1), :], -1), (SLOTS, SLOTS))
        source_t, target_t = source.T, target.T
        for j in range(NODES // SLOTS):
            columns = pl.ds(j * SLOTS, SLOTS)
            from_ = jnp.where(source_t == lane + j * SLOTS, 1.0, 0.0)
            to = jnp.where(target_t == lane + j * SLOTS, 1.0, 0.0)
            pick[here, columns] = (from_ + to).astype(BF16)
            pick_t[here, columns] = to.astype(BF16)
            spread[columns, here] = jnp.where(target == sub + j * SLOTS, 1.0, 0.0).astype(BF16)
        pair = trips[b]
        heads = jnp.where(pair[0:1, :] < alive, pair[0:1, :], -1)
        receive = jnp.where(heads == sub_wide, 1.0, 0.0).astype(BF16)
        sender = jnp.where(pair[1:2, :] == sub_wide, 1.0, 0.0).astype(BF16)
        links[r] = dot(receive, sender, 1, 1).astype(BF16)
        links_t[r] = dot(sender, receive, 1, 1).astype(BF16)

    for r in range(BLK):
        prepare(r)
    in_emb.wait()
    for copy in in_w:
        copy.wait()
    node_two = gather_two(node, node_one)
    cot_two = gather_two(cot, cot_one)
    for copy in gather_three(node, node_one, node_two):
        copy.wait_recv()

    tile_rows = lax.broadcasted_iota(jnp.int32, (TILE, WIDTH), 0)

    def forward(first_, last_):
        here = pl.ds(first_ * SLOTS, (last_ - first_) * SLOTS)
        tiles = [
            (r, i * TILE, pl.ds(r * SLOTS + i * TILE, TILE))
            for r in range(first_, last_)
            for i in range(SLOTS // TILE)
        ]
        tmp[here, :] = dot(pick[here, :], node[...], 1, 0)
        for r, at_, tile in tiles:
            flat = emb[block(r), pl.ds(at_, TILE), :].astype(F32)
            flat = jnp.where(tile_rows < count[block(r)] - at_, flat, 0.0)
            left[0, tile, :] = (flat + tmp[tile, :]).astype(BF16)
        fs[here, :] = dot(left[0, here, :], w[...], 1, 0)
        for _, _, tile in tiles:
            z = fs[tile, :]
            sig = 0.5 * jnp.tanh(0.5 * z) + 0.5
            zs = z * sig
            left[1, tile, :] = zs.astype(BF16)
            fs[tile, :] = sig + zs * (1.0 - sig)
        right[1, here, :] = dot(left[1, here, :], tw[...], 1, 0).astype(BF16)
        for r in range(first_, last_):
            rows_ = pl.ds(r * SLOTS, SLOTS)
            tmp[rows_, :] = dot(links[r], right[1, rows_, :], 1, 0)
        for r, at_, tile in tiles:
            v = (left[1, tile, :].astype(F32) + tmp[tile, :]).astype(BF16)
            vs[tile, :] = v
            flat = emb[block(r), pl.ds(at_, TILE), :].astype(F32)
            near[r, pl.ds(at_, TILE), :] = (flat + v.astype(F32)).astype(BF16)

    def hand_out(r, start=0, size=SLOTS):
        some = pl.ds(start, size)
        send(near.at[r, some], edges_out.at[g, some], peer(*ROUTE[r]))

    forward(0, 2)
    hand_out(0)
    hand_out(1)
    forward(2, BLK)
    cot_in_all = gather_three(cot, cot_one, cot_two)
    hand_out(6)
    fetch(near.at[7], edges_out.at[g])

    def unit(dc, half):
        for r in (2 + dc, 4 + dc):
            hand_out(r, half * (SLOTS // 2), SLOTS // 2)

    agg[...] = dot(spread[...], vs[...], 1, 0)
    for i in range(4):
        agg_sib_out[pl.ds(i * OWN, OWN)] = agg[rows(2 * i + 1 - c, OWN)].astype(BF16)
    agg_sib = send(agg_sib_out, agg_sib_in, peer(0, 1))

    for copy in cot_in_all:
        copy.wait_recv()
    tmp[...] = dot(pick_t[...], cot[...], 1, 0)
    for r in range(BLK):
        rows_ = pl.ds(r * SLOTS, SLOTS)
        dv = (tmp[rows_, :] * coef).astype(BF16)
        dvs[rows_, :] = dv
        right[1, rows_, :] = dot(links_t[r], dv, 1, 0).astype(BF16)
    tmp[...] = dot(right[1], tw[...], 1, 1)
    for i in range(BLK * SLOTS // TILE):
        tile = pl.ds(i * TILE, TILE)
        du = dvs[tile, :].astype(F32) + tmp[tile, :]
        right[0, tile, :] = (du * fs[tile, :]).astype(BF16)

    gs_out[...] = dot(left[1 - c], right[1 - c], 0, 0).astype(BF16)
    grad_sib = send(gs_out, gs_in, peer(0, 1))
    grads[...] = dot(left[c], right[c], 0, 0)

    agg_sib.wait_recv()

    def chip_sum(dh, half=None):
        i = (h + dh) % 4
        n = OWN if half is None else OWN // 2
        o = 0 if half is None else half * (OWN // 2)
        mine = agg[pl.ds(pl.multiple_of((2 * i + c) * OWN + o, n), n)]
        return mine + agg_sib_in[pl.ds(pl.multiple_of(i * OWN + o, n), n)].astype(F32)

    for i in range(2):
        agg_one_out[i] = chip_sum(2, i).astype(BF16)
    agg_one = [send(agg_one_out.at[0], agg_one_in.at[0], peer(1, 0)),
               send(agg_one_out.at[1], agg_one_in.at[1], peer(3, 0))]

    grad_sib.wait_recv()
    grads[...] += gs_in[...].astype(F32)
    red_one = []
    for i in (1, 2, 3):
        r1_out[i - 1] = grads[rows((p + i) % 4, 128), :].astype(BF16)
        red_one.append(send(r1_out.at[i - 1], r1_in.at[i - 1], first(i)))
    for copy in red_one:
        copy.wait_recv()
    r1_sum[...] = (
        grads[rows(p, 128), :] + r1_in[0].astype(F32) + r1_in[1].astype(F32) + r1_in[2].astype(F32)
    )
    red_two = []
    for i in (1, 2, 3):
        r2_out[i - 1] = r1_sum[rows((s + i) % 4, 32), :].astype(BF16)
        red_two.append(send(r2_out.at[i - 1], r2_in.at[i - 1], second(i)))
    for copy in red_two:
        copy.wait_recv()
    r2 = r1_sum[rows(s, 32), :]
    for i in range(3):
        r2 = r2 + r2_in[i].astype(F32)
    for i in range(4):
        r3_out[i] = r2[:, i * 128 : (i + 1) * 128]
    red_three = []
    for i in (1, 2, 3):
        k = (zl + i) % 4
        r3_in[i + 2] = r3_out[k].astype(BF16)
        red_three.append(send(r3_in.at[i + 2], r3_in.at[i - 1], third(i)))
    unit(0, 0)

    for i in range(2):
        agg_one[i].wait_recv()
        agg_two_out[i, pl.ds(i * (OWN // 2), OWN // 2)] = (
            chip_sum((1, 3)[i], i) + agg_one_in[i].astype(F32)
        ).astype(BF16)
        agg_two_out[i, pl.ds((1 - i) * (OWN // 2), OWN // 2)] = chip_sum((1, 3)[i], 1 - i).astype(BF16)

    for copy in red_three:
        copy.wait_recv()
    r3 = r3_out[zl]
    for i in range(3):
        r3 = r3 + r3_in[i].astype(F32)
    r4[h] = r3.astype(BF16)
    red_four = [send(r4.at[h], r4.at[h], peer(i, 0)) for i in (1, 2, 3)]
    agg_two = [send(agg_two_out.at[i], agg_two_in.at[i], peer((1, 3)[i], 0)) for i in range(2)]
    unit(0, 1)

    for copy in red_four:
        copy.wait_recv()
    four = r4[0].astype(F32) + r4[1].astype(F32) + r4[2].astype(F32) + r4[3].astype(F32)
    block_ = pl.ds(pl.multiple_of(p * 128 + s * 32, 32), 32)
    band = pl.ds(pl.multiple_of(zl * 128, 128), 128)
    total[c, block_, band] = four.astype(BF16)

    def spread_out(region, partner):
        return [send(total.at[region], total.at[region], partner(i)) for i in (1, 2, 3)]

    back = spread_out((c, block_, band), third)
    unit(1, 0)
    unit(1, 1)

    for copy in agg_two:
        copy.wait_recv()
    nodes_out[...] = (
        node[own].astype(F32)
        + 0.25 * (chip_sum(0) + agg_two_in[0].astype(F32) + agg_two_in[1].astype(F32))
    ).astype(BF16)

    for copy in back:
        copy.wait_recv()
    for copy in spread_out((c, block_), second):
        copy.wait_recv()
    back_one = spread_out((c, rows(p, 128)), first)
    beside = [send(total.at[c, rows(p, 128)], total.at[c, rows(p, 128)], peer(0, 1))]
    for i, copy in enumerate(back_one):
        copy.wait_recv()
        held = total.at[c, rows((p + 3 - i) % 4, 128)]
        beside.append(send(held, held, peer(0, 1)))
    for copy in beside:
        copy.wait_recv()
    grads_out[...] = total[...]
    finish()


def shards(
    node_emb,
    edge_emb,
    edge_source,
    edge_target,
    valid_count,
    triplets,
    send_order,
    w_edge,
    triplet_weight,
    node_embedding_cotangent,
):
    coef = 0.25 / math.sqrt(lax.axis_size("dp") * NODES)
    anywhere = pl.BlockSpec(memory_space=pl.ANY)
    smem = pl.BlockSpec(memory_space=pltpu.SMEM)
    vmem = pl.BlockSpec(memory_space=pltpu.VMEM)
    edges = BLK * SLOTS

    def scratch(*shape, dtype=BF16):
        return pltpu.VMEM(shape, dtype)

    nodes, packed, grads = pl.pallas_call(
        lambda *refs: kernel(coef, *refs),
        out_shape=(
            jax.ShapeDtypeStruct((OWN, WIDTH), BF16),
            jax.ShapeDtypeStruct((BLK, SLOTS, WIDTH), BF16),
            jax.ShapeDtypeStruct((2, WIDTH, WIDTH), BF16),
        ),
        in_specs=[smem, smem] + [anywhere] * 8,
        out_specs=(vmem, anywhere, vmem),
        scratch_shapes=[
            scratch(BLK, SLOTS, dtype=jnp.int32),
            scratch(BLK, SLOTS, dtype=jnp.int32),
            scratch(BLK, 2, 2 * SLOTS, dtype=jnp.int32),
            scratch(NODES, WIDTH),
            scratch(NODES, WIDTH),
            scratch(BLK, SLOTS, WIDTH),
            scratch(WIDTH, WIDTH),
            scratch(WIDTH, WIDTH),
            scratch(edges, NODES),
            scratch(edges, NODES),
            scratch(NODES, edges),
            scratch(BLK, SLOTS, SLOTS),
            scratch(BLK, SLOTS, SLOTS),
            scratch(2, edges, WIDTH),
            scratch(2, edges, WIDTH),
            scratch(edges, WIDTH, dtype=F32),
            scratch(edges, WIDTH),
            scratch(edges, WIDTH),
            scratch(edges, WIDTH, dtype=F32),
            scratch(BLK, SLOTS, WIDTH),
            scratch(4 * OWN, WIDTH),
            scratch(4 * OWN, WIDTH),
            scratch(NODES, WIDTH, dtype=F32),
            scratch(2, OWN // 2, WIDTH),
            scratch(2, OWN // 2, WIDTH),
            scratch(2, OWN, WIDTH),
            scratch(2, OWN, WIDTH),
            scratch(WIDTH, WIDTH, dtype=F32),
            scratch(WIDTH, WIDTH),
            scratch(WIDTH, WIDTH),
            scratch(3, 128, WIDTH),
            scratch(3, 128, WIDTH),
            scratch(128, WIDTH, dtype=F32),
            scratch(3, 32, WIDTH),
            scratch(3, 32, WIDTH),
            scratch(4, 32, 128, dtype=F32),
            scratch(6, 32, 128),
            scratch(4, 32, 128),
            scratch(2, WIDTH, WIDTH),
            pltpu.SemaphoreType.DMA((9,)),
            pltpu.SemaphoreType.DMA((64,)),
            pltpu.SemaphoreType.DMA((64,)),
        ],
        compiler_params=pltpu.CompilerParams(
            collective_id=0, has_side_effects=True, vmem_limit_bytes=62 << 20
        ),
    )(
        send_order.reshape(BLK),
        valid_count.reshape(BLK),
        edge_source[0],
        edge_target[0],
        triplets[0],
        node_emb[0],
        node_embedding_cotangent[0],
        edge_emb[0],
        w_edge,
        triplet_weight,
    )
    return (nodes[None], packed[None], grads[0].astype(F32), grads[1].astype(F32))


def solution(mesh):
    in_specs = (
        P("dp", "graph", None),
        P("dp", "graph", None, None),
        P("dp", "graph", None),
        P("dp", "graph", None),
        P("dp", "graph"),
        P("dp", "graph", None, None),
        P("dp", "graph", None),
        P(),
        P(),
        P("dp", "graph", None),
    )
    out_specs = (P("dp", "graph", None), P("dp", "graph", None, None), P(), P())
    return jax.shard_map(shards, mesh=mesh, in_specs=in_specs, out_specs=out_specs, check_vma=False)
```

```python
import math

import jax
import jax.numpy as jnp
from jax import lax
from jax.experimental import pallas as pl
from jax.experimental.pallas import tpu as pltpu
from jax.sharding import PartitionSpec as P

MESH = pl.DeviceIdType.MESH
F32, BF16 = jnp.float32, jnp.bfloat16

TILE = 32
BLK, SLOTS, WIDTH, NODES = 8, 128, 512, 512
OWN = NODES // 8
ROUTE = ((2, 0), (2, 1), (1, 0), (1, 1), (3, 0), (3, 1), (0, 1), (0, 0))


class Copy:
    def __init__(self, copy, remote=True):
        self.copy, self.remote, self.got, self.left = copy, remote, False, False

    def wait_recv(self):
        if not self.got:
            self.copy.wait_recv() if self.remote else self.copy.wait()
            self.got = True

    wait = wait_recv

    def wait_send(self):
        if self.remote and not self.left:
            self.copy.wait_send()
            self.left = True


def dot(a, b, ca, cb):
    return lax.dot_general(a, b, (((ca,), (cb,)), ((), ())), preferred_element_type=F32)


def kernel(
    coef,
    order,
    count,
    src_in,
    dst_in,
    trip_in,
    node_in,
    cot_in,
    emb_in,
    w_in,
    tw_in,
    nodes_out,
    edges_out,
    grads_out,
    srcs,
    dsts,
    trips,
    node,
    cot,
    emb,
    w,
    tw,
    pick,
    pick_t,
    spread,
    links,
    links_t,
    left,
    right,
    fs,
    vs,
    dvs,
    tmp,
    near,
    agg_sib_out,
    agg_sib_in,
    agg,
    agg_one_out,
    agg_one_in,
    agg_two_out,
    agg_two_in,
    grads,
    gs_out,
    gs_in,
    r1_out,
    r1_in,
    r1_sum,
    r2_out,
    r2_in,
    r3_out,
    r3_in,
    r4,
    total,
    lsem,
    ssem,
    rsem,
):
    g, d = lax.axis_index("graph"), lax.axis_index("dp")
    h, c = g // 2, g % 2
    y, zl, x = d // 16, (d // 4) % 4, d % 4

    def chip(dh):
        return (h + dh * (1 + 2 * c)) % 4

    def peer(dh, dc):
        return (d, chip(dh) * 2 + (c + dc) % 2)

    def at(yy, zz, xx):
        return (((yy % 4) * 4 + zz % 4) * 4 + xx % 4, g)

    def first(i):
        return at(y + i * c, zl, x + i * (1 - c))

    def second(i):
        return at(y + i * (1 - c), zl, x + i * c)

    def third(i):
        return at(y, zl + i, x)

    p = x * (1 - c) + y * c
    s = y * (1 - c) + x * c

    used = [0]
    every = []

    def finish():
        for copy in every:
            copy.wait_recv()
        for copy in every:
            copy.wait_send()


    def send(source, target, device):
        i = used[0]
        used[0] += 1
        copy = pltpu.make_async_remote_copy(
            src_ref=source,
            dst_ref=target,
            send_sem=ssem.at[i],
            recv_sem=rsem.at[i],
            device_id=device,
            device_id_type=MESH,
        )
        copy.start()
        copy = Copy(copy)
        every.append(copy)
        return copy

    local = [0]

    def fetch(source, target):
        copy = pltpu.make_async_copy(source, target, lsem.at[local[0]])
        local[0] += 1
        copy.start()
        copy = Copy(copy, False)
        every.append(copy)
        return copy

    def rows(i, n):
        return pl.ds(pl.multiple_of(i * n, n), n)

    own = rows(g, OWN)
    in_node = fetch(node_in, node.at[own])
    in_ids = [fetch(src_in, srcs), fetch(dst_in, dsts), fetch(trip_in, trips)]
    in_cot = fetch(cot_in, cot.at[own])
    in_emb = fetch(emb_in, emb)
    in_w = [fetch(w_in, w), fetch(tw_in, tw)]

    partners = [peer(0, 1), peer(1, 0), peer(1, 1), peer(3, 0), peer(3, 1), peer(2, 0), peer(2, 1)]
    for i in (1, 2, 3):
        partners += [first(i), second(i), third(i)]
    barrier = pltpu.get_barrier_semaphore()
    for partner in partners:
        pl.semaphore_signal(barrier, 1, device_id=partner, device_id_type=MESH)
    pl.semaphore_wait(barrier, len(partners))


    def part(ref, dh, dc, half=None):
        base = (chip(dh) * 2 + (c + dc) % 2) * OWN
        if half is None:
            return ref.at[pl.ds(pl.multiple_of(base, OWN), OWN)]
        return ref.at[pl.ds(pl.multiple_of(base + half * (OWN // 2), OWN // 2), OWN // 2)]

    def gather_one(ref):
        return [send(part(ref, 0, 0), part(ref, 0, 0), peer(*to)) for to in ((1, 0), (3, 0), (0, 1))]

    def gather_two(ref, one):
        up, down, beside = one
        up.wait_recv()
        two = [
            send(part(ref, 3, 0, 0), part(ref, 3, 0, 0), peer(1, 0)),
            send(part(ref, 3, 0), part(ref, 3, 0), peer(0, 1)),
        ]
        down.wait_recv()
        two += [
            send(part(ref, 1, 0, 1), part(ref, 1, 0, 1), peer(3, 0)),
            send(part(ref, 1, 0), part(ref, 1, 0), peer(0, 1)),
        ]
        return two

    def gather_three(ref, one, two):
        two[0].wait_recv()
        three = [send(part(ref, 2, 0, 0), part(ref, 2, 0, 0), peer(0, 1))]
        two[2].wait_recv()
        three += [send(part(ref, 2, 0, 1), part(ref, 2, 0, 1), peer(0, 1))]
        return [one[2], two[1], two[3]] + three

    in_node.wait()
    node_one = gather_one(node)
    in_cot.wait()
    cot_one = gather_one(cot)
    for copy in in_ids:
        copy.wait()

    lane = lax.broadcasted_iota(jnp.int32, (SLOTS, SLOTS), 1)
    sub = lax.broadcasted_iota(jnp.int32, (SLOTS, SLOTS), 0)
    sub_wide = lax.broadcasted_iota(jnp.int32, (SLOTS, 2 * SLOTS), 0)

    def block(r):
        dh, dc = ROUTE[r]
        return order[chip(dh) * 2 + (c + dc) % 2]

    def prepare(r):
        b = block(r)
        alive = count[b]
        here = pl.ds(r * SLOTS, SLOTS)
        live = lax.broadcasted_iota(jnp.int32, (1, SLOTS), 1) < alive
        source = jnp.broadcast_to(jnp.where(live, srcs[pl.ds(b, 1), :], -1), (SLOTS, SLOTS))
        target = jnp.broadcast_to(jnp.where(live, dsts[pl.ds(b, 1), :], -1), (SLOTS, SLOTS))
        source_t, target_t = source.T, target.T
        for j in range(NODES // SLOTS):
            columns = pl.ds(j * SLOTS, SLOTS)
            from_ = jnp.where(source_t == lane + j * SLOTS, 1.0, 0.0)
            to = jnp.where(target_t == lane + j * SLOTS, 1.0, 0.0)
            pick[here, columns] = (from_ + to).astype(BF16)
            pick_t[here, columns] = to.astype(BF16)
            spread[columns, here] = jnp.where(target == sub + j * SLOTS, 1.0, 0.0).astype(BF16)
        pair = trips[b]
        heads = jnp.where(pair[0:1, :] < alive, pair[0:1, :], -1)
        receive = jnp.where(heads == sub_wide, 1.0, 0.0).astype(BF16)
        sender = jnp.where(pair[1:2, :] == sub_wide, 1.0, 0.0).astype(BF16)
        links[r] = dot(receive, sender, 1, 1).astype(BF16)
        links_t[r] = dot(sender, receive, 1, 1).astype(BF16)

    for r in range(BLK):
        prepare(r)
    in_emb.wait()
    for copy in in_w:
        copy.wait()
    node_two = gather_two(node, node_one)
    cot_two = gather_two(cot, cot_one)
    for copy in gather_three(node, node_one, node_two):
        copy.wait_recv()

    tile_rows = lax.broadcasted_iota(jnp.int32, (TILE, WIDTH), 0)

    def forward(first_, last_):
        here = pl.ds(first_ * SLOTS, (last_ - first_) * SLOTS)
        tiles = [
            (r, i * TILE, pl.ds(r * SLOTS + i * TILE, TILE))
            for r in range(first_, last_)
            for i in range(SLOTS // TILE)
        ]
        tmp[here, :] = dot(pick[here, :], node[...], 1, 0)
        for r, at_, tile in tiles:
            flat = emb[block(r), pl.ds(at_, TILE), :].astype(F32)
            flat = jnp.where(tile_rows < count[block(r)] - at_, flat, 0.0)
            left[0, tile, :] = (flat + tmp[tile, :]).astype(BF16)
        fs[here, :] = dot(left[0, here, :], w[...], 1, 0)
        for _, _, tile in tiles:
            z = fs[tile, :]
            sig = 0.5 * jnp.tanh(0.5 * z) + 0.5
            zs = z * sig
            left[1, tile, :] = zs.astype(BF16)
            fs[tile, :] = sig + zs * (1.0 - sig)
        right[1, here, :] = dot(left[1, here, :], tw[...], 1, 0).astype(BF16)
        for r in range(first_, last_):
            rows_ = pl.ds(r * SLOTS, SLOTS)
            tmp[rows_, :] = dot(links[r], right[1, rows_, :], 1, 0)
        for r, at_, tile in tiles:
            v = (left[1, tile, :].astype(F32) + tmp[tile, :]).astype(BF16)
            vs[tile, :] = v
            flat = emb[block(r), pl.ds(at_, TILE), :].astype(F32)
            near[r, pl.ds(at_, TILE), :] = (flat + v.astype(F32)).astype(BF16)

    def hand_out(r, start=0, size=SLOTS):
        some = pl.ds(start, size)
        send(near.at[r, some], edges_out.at[g, some], peer(*ROUTE[r]))

    for r in range(2):
        forward(r, r + 1)
        hand_out(r)
    forward(2, BLK)
    cot_in_all = gather_three(cot, cot_one, cot_two)
    hand_out(6)
    fetch(near.at[7], edges_out.at[g])

    def unit(dc, half):
        for r in (2 + dc, 4 + dc):
            hand_out(r, half * (SLOTS // 2), SLOTS // 2)

    agg[...] = dot(spread[...], vs[...], 1, 0)
    for i in range(4):
        agg_sib_out[pl.ds(i * OWN, OWN)] = agg[rows(2 * i + 1 - c, OWN)].astype(BF16)
    agg_sib = send(agg_sib_out, agg_sib_in, peer(0, 1))

    for copy in cot_in_all:
        copy.wait_recv()
    tmp[...] = dot(pick_t[...], cot[...], 1, 0)
    for r in range(BLK):
        rows_ = pl.ds(r * SLOTS, SLOTS)
        dv = (tmp[rows_, :] * coef).astype(BF16)
        dvs[rows_, :] = dv
        right[1, rows_, :] = dot(links_t[r], dv, 1, 0).astype(BF16)
    tmp[...] = dot(right[1], tw[...], 1, 1)
    for i in range(BLK * SLOTS // TILE):
        tile = pl.ds(i * TILE, TILE)
        du = dvs[tile, :].astype(F32) + tmp[tile, :]
        right[0, tile, :] = (du * fs[tile, :]).astype(BF16)

    gs_out[...] = dot(left[1 - c], right[1 - c], 0, 0).astype(BF16)
    grad_sib = send(gs_out, gs_in, peer(0, 1))
    grads[...] = dot(left[c], right[c], 0, 0)

    agg_sib.wait_recv()

    def chip_sum(dh, half=None):
        i = chip(dh)
        n = OWN if half is None else OWN // 2
        o = 0 if half is None else half * (OWN // 2)
        mine = agg[pl.ds(pl.multiple_of((2 * i + c) * OWN + o, n), n)]
        return mine + agg_sib_in[pl.ds(pl.multiple_of(i * OWN + o, n), n)].astype(F32)

    for i in range(2):
        agg_one_out[i] = chip_sum(2, i).astype(BF16)
    agg_one = [send(agg_one_out.at[0], agg_one_in.at[0], peer(1, 0)),
               send(agg_one_out.at[1], agg_one_in.at[1], peer(3, 0))]

    grad_sib.wait_recv()
    grads[...] += gs_in[...].astype(F32)
    red_one = []
    for i in (1, 2, 3):
        r1_out[i - 1] = grads[rows((p + i) % 4, 128), :].astype(BF16)
        red_one.append(send(r1_out.at[i - 1], r1_in.at[i - 1], first(i)))
    for copy in red_one:
        copy.wait_recv()
    r1_sum[...] = (
        grads[rows(p, 128), :] + r1_in[0].astype(F32) + r1_in[1].astype(F32) + r1_in[2].astype(F32)
    )
    red_two = []
    for i in (1, 2, 3):
        r2_out[i - 1] = r1_sum[rows((s + i) % 4, 32), :].astype(BF16)
        red_two.append(send(r2_out.at[i - 1], r2_in.at[i - 1], second(i)))
    for copy in red_two:
        copy.wait_recv()
    r2 = r1_sum[rows(s, 32), :]
    for i in range(3):
        r2 = r2 + r2_in[i].astype(F32)
    for i in range(4):
        r3_out[i] = r2[:, i * 128 : (i + 1) * 128]
    red_three = []
    for i in (1, 2, 3):
        k = (zl + i) % 4
        r3_in[i + 2] = r3_out[k].astype(BF16)
        red_three.append(send(r3_in.at[i + 2], r3_in.at[i - 1], third(i)))
    unit(0, 0)

    for i in range(2):
        agg_one[i].wait_recv()
        agg_two_out[i, pl.ds(i * (OWN // 2), OWN // 2)] = (
            chip_sum((1, 3)[i], i) + agg_one_in[i].astype(F32)
        ).astype(BF16)
        agg_two_out[i, pl.ds((1 - i) * (OWN // 2), OWN // 2)] = chip_sum((1, 3)[i], 1 - i).astype(BF16)

    for copy in red_three:
        copy.wait_recv()
    r3 = r3_out[zl]
    for i in range(3):
        r3 = r3 + r3_in[i].astype(F32)
    r4[h] = r3.astype(BF16)
    red_four = [send(r4.at[h], r4.at[h], peer(i, 0)) for i in (1, 2, 3)]
    agg_two = [send(agg_two_out.at[i], agg_two_in.at[i], peer((1, 3)[i], 0)) for i in range(2)]
    unit(0, 1)

    for copy in red_four:
        copy.wait_recv()
    four = r4[0].astype(F32) + r4[1].astype(F32) + r4[2].astype(F32) + r4[3].astype(F32)
    block_ = pl.ds(pl.multiple_of(p * 128 + s * 32, 32), 32)
    band = pl.ds(pl.multiple_of(zl * 128, 128), 128)
    total[c, block_, band] = four.astype(BF16)

    def spread_out(region, partner):
        return [send(total.at[region], total.at[region], partner(i)) for i in (1, 2, 3)]

    back = spread_out((c, block_, band), third)
    unit(1, 0)
    unit(1, 1)

    for copy in agg_two:
        copy.wait_recv()
    nodes_out[...] = (
        node[own].astype(F32)
        + 0.25 * (chip_sum(0) + agg_two_in[0].astype(F32) + agg_two_in[1].astype(F32))
    ).astype(BF16)

    for copy in back:
        copy.wait_recv()
    for copy in spread_out((c, block_), second):
        copy.wait_recv()
    back_one = spread_out((c, rows(p, 128)), first)
    beside = [send(total.at[c, rows(p, 128)], total.at[c, rows(p, 128)], peer(0, 1))]
    for i, copy in enumerate(back_one):
        copy.wait_recv()
        held = total.at[c, rows((p + 3 - i) % 4, 128)]
        beside.append(send(held, held, peer(0, 1)))
    for copy in beside:
        copy.wait_recv()
    grads_out[...] = total[...]
    finish()


def finish_kernel(nodes, edges, grads, nodes_out, edges_out, edge_grad, trip_grad, held, kept, rows, wide, sem):
    used = [0]

    def move(source, target):
        copy = pltpu.make_async_copy(source, target, sem.at[used[0]])
        used[0] += 1
        copy.start()
        return copy

    loads = [move(grads.at[i], held.at[i]) for i in range(2)]
    parts = [pl.ds(i * 2, 2) for i in range(BLK // 2)]
    blocks = [move(edges.at[part], kept.at[part]) for part in parts]
    own = move(nodes, rows)
    stores = []
    for i, out in enumerate((edge_grad, trip_grad)):
        loads[i].wait()
        for j in range(WIDTH // 64):
            wide[i, pl.ds(j * 64, 64), :] = held[i, pl.ds(j * 64, 64), :].astype(F32)
        stores.append(move(wide.at[i], out))
        for k in (2 * i, 2 * i + 1):
            blocks[k].wait()
            stores.append(move(kept.at[parts[k]], edges_out.at[parts[k]]))
    own.wait()
    stores.append(move(rows, nodes_out))
    for copy in stores:
        copy.wait()


def shards(
    node_emb,
    edge_emb,
    edge_source,
    edge_target,
    valid_count,
    triplets,
    send_order,
    w_edge,
    triplet_weight,
    node_embedding_cotangent,
):
    coef = 0.25 / math.sqrt(lax.axis_size("dp") * NODES)
    anywhere = pl.BlockSpec(memory_space=pl.ANY)
    smem = pl.BlockSpec(memory_space=pltpu.SMEM)
    vmem = pl.BlockSpec(memory_space=pltpu.VMEM)
    edges = BLK * SLOTS

    def scratch(*shape, dtype=BF16):
        return pltpu.VMEM(shape, dtype)

    nodes, packed, grads = pl.pallas_call(
        lambda *refs: kernel(coef, *refs),
        out_shape=(
            jax.ShapeDtypeStruct((OWN, WIDTH), BF16),
            jax.ShapeDtypeStruct((BLK, SLOTS, WIDTH), BF16),
            jax.ShapeDtypeStruct((2, WIDTH, WIDTH), BF16),
        ),
        in_specs=[smem, smem] + [anywhere] * 8,
        out_specs=(vmem, anywhere, vmem),
        scratch_shapes=[
            scratch(BLK, SLOTS, dtype=jnp.int32),
            scratch(BLK, SLOTS, dtype=jnp.int32),
            scratch(BLK, 2, 2 * SLOTS, dtype=jnp.int32),
            scratch(NODES, WIDTH),
            scratch(NODES, WIDTH),
            scratch(BLK, SLOTS, WIDTH),
            scratch(WIDTH, WIDTH),
            scratch(WIDTH, WIDTH),
            scratch(edges, NODES),
            scratch(edges, NODES),
            scratch(NODES, edges),
            scratch(BLK, SLOTS, SLOTS),
            scratch(BLK, SLOTS, SLOTS),
            scratch(2, edges, WIDTH),
            scratch(2, edges, WIDTH),
            scratch(edges, WIDTH, dtype=F32),
            scratch(edges, WIDTH),
            scratch(edges, WIDTH),
            scratch(edges, WIDTH, dtype=F32),
            scratch(BLK, SLOTS, WIDTH),
            scratch(4 * OWN, WIDTH),
            scratch(4 * OWN, WIDTH),
            scratch(NODES, WIDTH, dtype=F32),
            scratch(2, OWN // 2, WIDTH),
            scratch(2, OWN // 2, WIDTH),
            scratch(2, OWN, WIDTH),
            scratch(2, OWN, WIDTH),
            scratch(WIDTH, WIDTH, dtype=F32),
            scratch(WIDTH, WIDTH),
            scratch(WIDTH, WIDTH),
            scratch(3, 128, WIDTH),
            scratch(3, 128, WIDTH),
            scratch(128, WIDTH, dtype=F32),
            scratch(3, 32, WIDTH),
            scratch(3, 32, WIDTH),
            scratch(4, 32, 128, dtype=F32),
            scratch(6, 32, 128),
            scratch(4, 32, 128),
            scratch(2, WIDTH, WIDTH),
            pltpu.SemaphoreType.DMA((9,)),
            pltpu.SemaphoreType.DMA((64,)),
            pltpu.SemaphoreType.DMA((64,)),
        ],
        compiler_params=pltpu.CompilerParams(
            collective_id=0, has_side_effects=True, vmem_limit_bytes=62 << 20
        ),
    )(
        send_order.reshape(BLK),
        valid_count.reshape(BLK),
        edge_source[0],
        edge_target[0],
        triplets[0],
        node_emb[0],
        node_embedding_cotangent[0],
        edge_emb[0],
        w_edge,
        triplet_weight,
    )
    nodes, packed, edge_grad, trip_grad = pl.pallas_call(
        finish_kernel,
        out_shape=(
            jax.ShapeDtypeStruct((OWN, WIDTH), BF16),
            jax.ShapeDtypeStruct((BLK, SLOTS, WIDTH), BF16),
            jax.ShapeDtypeStruct((WIDTH, WIDTH), F32),
            jax.ShapeDtypeStruct((WIDTH, WIDTH), F32),
        ),
        in_specs=[anywhere] * 3,
        out_specs=(anywhere,) * 4,
        scratch_shapes=[
            scratch(2, WIDTH, WIDTH),
            scratch(BLK, SLOTS, WIDTH),
            scratch(OWN, WIDTH),
            scratch(2, WIDTH, WIDTH, dtype=F32),
            pltpu.SemaphoreType.DMA((14,)),
        ],
        compiler_params=pltpu.CompilerParams(vmem_limit_bytes=62 << 20),
    )(nodes, packed, grads)
    return (nodes[None], packed[None], edge_grad, trip_grad)


def solution(mesh):
    in_specs = (
        P("dp", "graph", None),
        P("dp", "graph", None, None),
        P("dp", "graph", None),
        P("dp", "graph", None),
        P("dp", "graph"),
        P("dp", "graph", None, None),
        P("dp", "graph", None),
        P(),
        P(),
        P("dp", "graph", None),
    )
    out_specs = (P("dp", "graph", None), P("dp", "graph", None, None), P(), P())
    return jax.shard_map(shards, mesh=mesh, in_specs=in_specs, out_specs=out_specs, check_vma=False)
```

```python
import math

import jax
import jax.numpy as jnp
from jax import lax
from jax.experimental import pallas as pl
from jax.experimental.pallas import tpu as pltpu
from jax.sharding import PartitionSpec as P

MESH = pl.DeviceIdType.MESH
F32, BF16 = jnp.float32, jnp.bfloat16

TILE = 32
BLK, SLOTS, WIDTH, NODES = 8, 128, 512, 512
OWN = NODES // 8
ROUTE = ((2, 0), (2, 1), (1, 0), (1, 1), (3, 0), (3, 1), (0, 1), (0, 0))


class Copy:
    def __init__(self, copy, remote=True):
        self.copy, self.remote, self.got, self.left = copy, remote, False, False

    def wait_recv(self):
        if not self.got:
            self.copy.wait_recv() if self.remote else self.copy.wait()
            self.got = True

    wait = wait_recv

    def wait_send(self):
        if self.remote and not self.left:
            self.copy.wait_send()
            self.left = True


def dot(a, b, ca, cb):
    return lax.dot_general(a, b, (((ca,), (cb,)), ((), ())), preferred_element_type=F32)


def kernel(
    coef,
    order,
    count,
    src_in,
    dst_in,
    trip_in,
    node_in,
    cot_in,
    emb_in,
    w_in,
    tw_in,
    nodes_out,
    edges_out,
    grads_out,
    srcs,
    dsts,
    trips,
    node,
    cot,
    emb,
    w,
    tw,
    pick,
    pick_t,
    spread,
    links,
    links_t,
    left,
    right,
    fs,
    vs,
    dvs,
    tmp,
    near,
    agg_sib_out,
    agg_sib_in,
    agg,
    agg_one_out,
    agg_one_in,
    agg_two_out,
    agg_two_in,
    grads,
    gs_out,
    gs_in,
    r1_out,
    r1_in,
    r1_sum,
    r2_out,
    r2_in,
    r3_out,
    r3_in,
    r4,
    total,
    lsem,
    ssem,
    rsem,
):
    g, d = lax.axis_index("graph"), lax.axis_index("dp")
    h, c = g // 2, g % 2
    y, zl, x = d // 16, (d // 4) % 4, d % 4

    def chip(dh):
        return (h + dh * (1 + 2 * c)) % 4

    def peer(dh, dc):
        return (d, chip(dh) * 2 + (c + dc) % 2)

    def at(yy, zz, xx):
        return (((yy % 4) * 4 + zz % 4) * 4 + xx % 4, g)

    def first(i):
        return at(y + i * c, zl, x + i * (1 - c))

    def second(i):
        return at(y + i * (1 - c), zl, x + i * c)

    def third(i):
        return at(y, zl + i, x)

    p = x * (1 - c) + y * c
    s = y * (1 - c) + x * c

    used = [0]
    every = []

    def finish():
        for copy in every:
            copy.wait_recv()
        for copy in every:
            copy.wait_send()


    def send(source, target, device):
        i = used[0]
        used[0] += 1
        copy = pltpu.make_async_remote_copy(
            src_ref=source,
            dst_ref=target,
            send_sem=ssem.at[i],
            recv_sem=rsem.at[i],
            device_id=device,
            device_id_type=MESH,
        )
        copy.start()
        copy = Copy(copy)
        every.append(copy)
        return copy

    local = [0]

    def fetch(source, target):
        copy = pltpu.make_async_copy(source, target, lsem.at[local[0]])
        local[0] += 1
        copy.start()
        copy = Copy(copy, False)
        every.append(copy)
        return copy

    def rows(i, n):
        return pl.ds(pl.multiple_of(i * n, n), n)

    own = rows(g, OWN)
    in_node = fetch(node_in, node.at[own])
    in_ids = [fetch(src_in, srcs), fetch(dst_in, dsts), fetch(trip_in, trips)]
    in_cot = fetch(cot_in, cot.at[own])
    in_emb = fetch(emb_in, emb)
    in_w = [fetch(w_in, w), fetch(tw_in, tw)]

    partners = [peer(0, 1), peer(1, 0), peer(1, 1), peer(3, 0), peer(3, 1), peer(2, 0), peer(2, 1)]
    for i in (1, 2, 3):
        partners += [first(i), second(i), third(i)]
    barrier = pltpu.get_barrier_semaphore()
    for partner in partners:
        pl.semaphore_signal(barrier, 1, device_id=partner, device_id_type=MESH)
    pl.semaphore_wait(barrier, len(partners))


    def part(ref, dh, dc, half=None):
        base = (chip(dh) * 2 + (c + dc) % 2) * OWN
        if half is None:
            return ref.at[pl.ds(pl.multiple_of(base, OWN), OWN)]
        return ref.at[pl.ds(pl.multiple_of(base + half * (OWN // 2), OWN // 2), OWN // 2)]

    def gather_one(ref):
        return [send(part(ref, 0, 0), part(ref, 0, 0), peer(*to)) for to in ((1, 0), (3, 0), (0, 1))]

    def gather_two(ref, one):
        up, down, beside = one
        up.wait_recv()
        two = [
            send(part(ref, 3, 0, 0), part(ref, 3, 0, 0), peer(1, 0)),
            send(part(ref, 3, 0), part(ref, 3, 0), peer(0, 1)),
        ]
        down.wait_recv()
        two += [
            send(part(ref, 1, 0, 1), part(ref, 1, 0, 1), peer(3, 0)),
            send(part(ref, 1, 0), part(ref, 1, 0), peer(0, 1)),
        ]
        return two

    def gather_three(ref, one, two):
        two[0].wait_recv()
        three = [send(part(ref, 2, 0, 0), part(ref, 2, 0, 0), peer(0, 1))]
        two[2].wait_recv()
        three += [send(part(ref, 2, 0, 1), part(ref, 2, 0, 1), peer(0, 1))]
        return [one[2], two[1], two[3]] + three

    in_node.wait()
    node_one = gather_one(node)
    in_cot.wait()
    cot_one = gather_one(cot)
    for copy in in_ids:
        copy.wait()

    lane = lax.broadcasted_iota(jnp.int32, (SLOTS, SLOTS), 1)
    sub = lax.broadcasted_iota(jnp.int32, (SLOTS, SLOTS), 0)
    sub_wide = lax.broadcasted_iota(jnp.int32, (SLOTS, 2 * SLOTS), 0)

    def block(r):
        dh, dc = ROUTE[r]
        return order[chip(dh) * 2 + (c + dc) % 2]

    def prepare(r):
        b = block(r)
        alive = count[b]
        here = pl.ds(r * SLOTS, SLOTS)
        live = lax.broadcasted_iota(jnp.int32, (1, SLOTS), 1) < alive
        source = jnp.broadcast_to(jnp.where(live, srcs[pl.ds(b, 1), :], -1), (SLOTS, SLOTS))
        target = jnp.broadcast_to(jnp.where(live, dsts[pl.ds(b, 1), :], -1), (SLOTS, SLOTS))
        source_t, target_t = source.T, target.T
        for j in range(NODES // SLOTS):
            columns = pl.ds(j * SLOTS, SLOTS)
            from_ = jnp.where(source_t == lane + j * SLOTS, 1.0, 0.0)
            to = jnp.where(target_t == lane + j * SLOTS, 1.0, 0.0)
            pick[here, columns] = (from_ + to).astype(BF16)
            pick_t[here, columns] = to.astype(BF16)
            spread[columns, here] = jnp.where(target == sub + j * SLOTS, 1.0, 0.0).astype(BF16)
        pair = trips[b]
        heads = jnp.where(pair[0:1, :] < alive, pair[0:1, :], -1)
        receive = jnp.where(heads == sub_wide, 1.0, 0.0).astype(BF16)
        sender = jnp.where(pair[1:2, :] == sub_wide, 1.0, 0.0).astype(BF16)
        links[r] = dot(receive, sender, 1, 1).astype(BF16)
        links_t[r] = dot(sender, receive, 1, 1).astype(BF16)

    for r in range(BLK):
        prepare(r)
    in_emb.wait()
    for copy in in_w:
        copy.wait()
    node_two = gather_two(node, node_one)
    cot_two = gather_two(cot, cot_one)
    for copy in gather_three(node, node_one, node_two):
        copy.wait_recv()

    tile_rows = lax.broadcasted_iota(jnp.int32, (TILE, WIDTH), 0)

    def forward(first_, last_):
        here = pl.ds(first_ * SLOTS, (last_ - first_) * SLOTS)
        tiles = [
            (r, i * TILE, pl.ds(r * SLOTS + i * TILE, TILE))
            for r in range(first_, last_)
            for i in range(SLOTS // TILE)
        ]
        tmp[here, :] = dot(pick[here, :], node[...], 1, 0)
        for r, at_, tile in tiles:
            flat = emb[block(r), pl.ds(at_, TILE), :].astype(F32)
            flat = jnp.where(tile_rows < count[block(r)] - at_, flat, 0.0)
            left[0, tile, :] = (flat + tmp[tile, :]).astype(BF16)
        fs[here, :] = dot(left[0, here, :], w[...], 1, 0)
        for _, _, tile in tiles:
            z = fs[tile, :]
            sig = 0.5 * jnp.tanh(0.5 * z) + 0.5
            zs = z * sig
            left[1, tile, :] = zs.astype(BF16)
            fs[tile, :] = sig + zs * (1.0 - sig)
        right[1, here, :] = dot(left[1, here, :], tw[...], 1, 0).astype(BF16)
        for r in range(first_, last_):
            rows_ = pl.ds(r * SLOTS, SLOTS)
            tmp[rows_, :] = dot(links[r], right[1, rows_, :], 1, 0)
        for r, at_, tile in tiles:
            v = (left[1, tile, :].astype(F32) + tmp[tile, :]).astype(BF16)
            vs[tile, :] = v
            flat = emb[block(r), pl.ds(at_, TILE), :].astype(F32)
            near[r, pl.ds(at_, TILE), :] = (flat + v.astype(F32)).astype(BF16)

    def hand_out(r, start=0, size=SLOTS):
        some = pl.ds(start, size)
        send(near.at[r, some], edges_out.at[g, some], peer(*ROUTE[r]))

    for r in range(2):
        forward(r, r + 1)
        hand_out(r)
    forward(2, BLK)
    cot_in_all = gather_three(cot, cot_one, cot_two)
    hand_out(6)
    fetch(near.at[7], edges_out.at[g])

    def unit(dc, half):
        for r in (2 + dc, 4 + dc):
            hand_out(r, half * (SLOTS // 2), SLOTS // 2)

    agg[...] = dot(spread[...], vs[...], 1, 0)
    for i in range(4):
        agg_sib_out[pl.ds(i * OWN, OWN)] = agg[rows(2 * i + 1 - c, OWN)].astype(BF16)
    agg_sib = send(agg_sib_out, agg_sib_in, peer(0, 1))

    for copy in cot_in_all:
        copy.wait_recv()
    tmp[...] = dot(pick_t[...], cot[...], 1, 0)
    for r in range(BLK):
        rows_ = pl.ds(r * SLOTS, SLOTS)
        dv = (tmp[rows_, :] * coef).astype(BF16)
        dvs[rows_, :] = dv
        right[1, rows_, :] = dot(links_t[r], dv, 1, 0).astype(BF16)
    tmp[...] = dot(right[1], tw[...], 1, 1)
    for i in range(BLK * SLOTS // TILE):
        tile = pl.ds(i * TILE, TILE)
        du = dvs[tile, :].astype(F32) + tmp[tile, :]
        right[0, tile, :] = (du * fs[tile, :]).astype(BF16)

    gs_out[...] = dot(left[1 - c], right[1 - c], 0, 0).astype(BF16)
    grad_sib = send(gs_out, gs_in, peer(0, 1))
    grads[...] = dot(left[c], right[c], 0, 0)

    agg_sib.wait_recv()

    def chip_sum(dh, half=None):
        i = chip(dh)
        n = OWN if half is None else OWN // 2
        o = 0 if half is None else half * (OWN // 2)
        mine = agg[pl.ds(pl.multiple_of((2 * i + c) * OWN + o, n), n)]
        return mine + agg_sib_in[pl.ds(pl.multiple_of(i * OWN + o, n), n)].astype(F32)

    for i in range(2):
        agg_one_out[i] = chip_sum(2, i).astype(BF16)
    agg_one = [send(agg_one_out.at[0], agg_one_in.at[0], peer(1, 0)),
               send(agg_one_out.at[1], agg_one_in.at[1], peer(3, 0))]

    grad_sib.wait_recv()
    grads[...] += gs_in[...].astype(F32)
    red_one = []
    for i in (1, 2, 3):
        r1_out[i - 1] = grads[rows((p + i) % 4, 128), :].astype(BF16)
        red_one.append(send(r1_out.at[i - 1], r1_in.at[i - 1], first(i)))
    for copy in red_one:
        copy.wait_recv()
    r1_sum[...] = (
        grads[rows(p, 128), :] + r1_in[0].astype(F32) + r1_in[1].astype(F32) + r1_in[2].astype(F32)
    )
    red_two = []
    for i in (1, 2, 3):
        r2_out[i - 1] = r1_sum[rows((s + i) % 4, 32), :].astype(BF16)
        red_two.append(send(r2_out.at[i - 1], r2_in.at[i - 1], second(i)))
    for copy in red_two:
        copy.wait_recv()
    r2 = r1_sum[rows(s, 32), :]
    for i in range(3):
        r2 = r2 + r2_in[i].astype(F32)
    for i in range(4):
        r3_out[i] = r2[:, i * 128 : (i + 1) * 128]
    red_three = []
    for i in (1, 2, 3):
        k = (zl + i) % 4
        r3_in[i + 2] = r3_out[k].astype(BF16)
        red_three.append(send(r3_in.at[i + 2], r3_in.at[i - 1], third(i)))
    unit(0, 0)

    for i in range(2):
        agg_one[i].wait_recv()
        agg_two_out[i, pl.ds(i * (OWN // 2), OWN // 2)] = (
            chip_sum((1, 3)[i], i) + agg_one_in[i].astype(F32)
        ).astype(BF16)
        agg_two_out[i, pl.ds((1 - i) * (OWN // 2), OWN // 2)] = chip_sum((1, 3)[i], 1 - i).astype(BF16)

    for copy in red_three:
        copy.wait_recv()
    r3 = r3_out[zl]
    for i in range(3):
        r3 = r3 + r3_in[i].astype(F32)
    r4[h] = r3.astype(BF16)
    red_four = [send(r4.at[h], r4.at[h], peer(i, 0)) for i in (1, 2, 3)]
    agg_two = [send(agg_two_out.at[i], agg_two_in.at[i], peer((1, 3)[i], 0)) for i in range(2)]
    unit(0, 1)

    for copy in red_four:
        copy.wait_recv()
    four = r4[0].astype(F32) + r4[1].astype(F32) + r4[2].astype(F32) + r4[3].astype(F32)
    block_ = pl.ds(pl.multiple_of(p * 128 + s * 32, 32), 32)
    band = pl.ds(pl.multiple_of(zl * 128, 128), 128)
    total[c, block_, band] = four.astype(BF16)

    def spread_out(region, partner):
        return [send(total.at[region], total.at[region], partner(i)) for i in (1, 2, 3)]

    back = spread_out((c, block_, band), third)
    unit(1, 0)
    unit(1, 1)

    for copy in back:
        copy.wait_recv()
    for copy in spread_out((c, block_), second):
        copy.wait_recv()
    back_one = spread_out((c, rows(p, 128)), first)
    beside = [send(total.at[c, rows(p, 128)], total.at[c, rows(p, 128)], peer(0, 1))]
    for copy in agg_two:
        copy.wait_recv()
    nodes_out[...] = (
        node[own].astype(F32)
        + 0.25 * (chip_sum(0) + agg_two_in[0].astype(F32) + agg_two_in[1].astype(F32))
    ).astype(BF16)

    for i, copy in enumerate(back_one):
        copy.wait_recv()
        held = total.at[c, rows((p + 3 - i) % 4, 128)]
        beside.append(send(held, held, peer(0, 1)))
    for copy in beside:
        copy.wait_recv()
    grads_out[...] = total[...]
    finish()


def finish_kernel(nodes, edges, grads, nodes_out, edges_out, edge_grad, trip_grad, held, kept, rows, wide, sem):
    used = [0]

    def move(source, target):
        copy = pltpu.make_async_copy(source, target, sem.at[used[0]])
        used[0] += 1
        copy.start()
        return copy

    loads = [move(grads.at[i], held.at[i]) for i in range(2)]
    parts = [pl.ds(i * 2, 2) for i in range(BLK // 2)]
    blocks = [move(edges.at[part], kept.at[part]) for part in parts]
    own = move(nodes, rows)
    stores = []
    for i, out in enumerate((edge_grad, trip_grad)):
        loads[i].wait()
        for j in range(WIDTH // 64):
            wide[i, pl.ds(j * 64, 64), :] = held[i, pl.ds(j * 64, 64), :].astype(F32)
        stores.append(move(wide.at[i], out))
        for k in (2 * i, 2 * i + 1):
            blocks[k].wait()
            stores.append(move(kept.at[parts[k]], edges_out.at[parts[k]]))
    own.wait()
    stores.append(move(rows, nodes_out))
    for copy in stores:
        copy.wait()


def shards(
    node_emb,
    edge_emb,
    edge_source,
    edge_target,
    valid_count,
    triplets,
    send_order,
    w_edge,
    triplet_weight,
    node_embedding_cotangent,
):
    coef = 0.25 / math.sqrt(lax.axis_size("dp") * NODES)
    anywhere = pl.BlockSpec(memory_space=pl.ANY)
    smem = pl.BlockSpec(memory_space=pltpu.SMEM)
    vmem = pl.BlockSpec(memory_space=pltpu.VMEM)
    edges = BLK * SLOTS

    def scratch(*shape, dtype=BF16):
        return pltpu.VMEM(shape, dtype)

    nodes, packed, grads = pl.pallas_call(
        lambda *refs: kernel(coef, *refs),
        out_shape=(
            jax.ShapeDtypeStruct((OWN, WIDTH), BF16),
            jax.ShapeDtypeStruct((BLK, SLOTS, WIDTH), BF16),
            jax.ShapeDtypeStruct((2, WIDTH, WIDTH), BF16),
        ),
        in_specs=[smem, smem] + [anywhere] * 8,
        out_specs=(vmem, anywhere, vmem),
        scratch_shapes=[
            scratch(BLK, SLOTS, dtype=jnp.int32),
            scratch(BLK, SLOTS, dtype=jnp.int32),
            scratch(BLK, 2, 2 * SLOTS, dtype=jnp.int32),
            scratch(NODES, WIDTH),
            scratch(NODES, WIDTH),
            scratch(BLK, SLOTS, WIDTH),
            scratch(WIDTH, WIDTH),
            scratch(WIDTH, WIDTH),
            scratch(edges, NODES),
            scratch(edges, NODES),
            scratch(NODES, edges),
            scratch(BLK, SLOTS, SLOTS),
            scratch(BLK, SLOTS, SLOTS),
            scratch(2, edges, WIDTH),
            scratch(2, edges, WIDTH),
            scratch(edges, WIDTH, dtype=F32),
            scratch(edges, WIDTH),
            scratch(edges, WIDTH),
            scratch(edges, WIDTH, dtype=F32),
            scratch(BLK, SLOTS, WIDTH),
            scratch(4 * OWN, WIDTH),
            scratch(4 * OWN, WIDTH),
            scratch(NODES, WIDTH, dtype=F32),
            scratch(2, OWN // 2, WIDTH),
            scratch(2, OWN // 2, WIDTH),
            scratch(2, OWN, WIDTH),
            scratch(2, OWN, WIDTH),
            scratch(WIDTH, WIDTH, dtype=F32),
            scratch(WIDTH, WIDTH),
            scratch(WIDTH, WIDTH),
            scratch(3, 128, WIDTH),
            scratch(3, 128, WIDTH),
            scratch(128, WIDTH, dtype=F32),
            scratch(3, 32, WIDTH),
            scratch(3, 32, WIDTH),
            scratch(4, 32, 128, dtype=F32),
            scratch(6, 32, 128),
            scratch(4, 32, 128),
            scratch(2, WIDTH, WIDTH),
            pltpu.SemaphoreType.DMA((9,)),
            pltpu.SemaphoreType.DMA((64,)),
            pltpu.SemaphoreType.DMA((64,)),
        ],
        compiler_params=pltpu.CompilerParams(
            collective_id=0, has_side_effects=True, vmem_limit_bytes=62 << 20
        ),
    )(
        send_order.reshape(BLK),
        valid_count.reshape(BLK),
        edge_source[0],
        edge_target[0],
        triplets[0],
        node_emb[0],
        node_embedding_cotangent[0],
        edge_emb[0],
        w_edge,
        triplet_weight,
    )
    nodes, packed, edge_grad, trip_grad = pl.pallas_call(
        finish_kernel,
        out_shape=(
            jax.ShapeDtypeStruct((OWN, WIDTH), BF16),
            jax.ShapeDtypeStruct((BLK, SLOTS, WIDTH), BF16),
            jax.ShapeDtypeStruct((WIDTH, WIDTH), F32),
            jax.ShapeDtypeStruct((WIDTH, WIDTH), F32),
        ),
        in_specs=[anywhere] * 3,
        out_specs=(anywhere,) * 4,
        scratch_shapes=[
            scratch(2, WIDTH, WIDTH),
            scratch(BLK, SLOTS, WIDTH),
            scratch(OWN, WIDTH),
            scratch(2, WIDTH, WIDTH, dtype=F32),
            pltpu.SemaphoreType.DMA((14,)),
        ],
        compiler_params=pltpu.CompilerParams(vmem_limit_bytes=62 << 20),
    )(nodes, packed, grads)
    return (nodes[None], packed[None], edge_grad, trip_grad)


def solution(mesh):
    in_specs = (
        P("dp", "graph", None),
        P("dp", "graph", None, None),
        P("dp", "graph", None),
        P("dp", "graph", None),
        P("dp", "graph"),
        P("dp", "graph", None, None),
        P("dp", "graph", None),
        P(),
        P(),
        P("dp", "graph", None),
    )
    out_specs = (P("dp", "graph", None), P("dp", "graph", None, None), P(), P())
    return jax.shard_map(shards, mesh=mesh, in_specs=in_specs, out_specs=out_specs, check_vma=False)
```
